32 devices in a mesh: ctx: 8 (over y, x, core), exp: 4 (over z).
Axes of the slice: x: 2, y: 2, z: 4, core: 2. Of those that a mesh axis runs over, the one named last changes fastest.
Arguments:
- queries: bfloat16 [4096, 4096], P('ctx', 'exp'), may hold values from -6 to 6
- keys: bfloat16 [4096, 256], P('ctx'), may hold values from -6 to 6
- values: bfloat16 [4096, 256], P('ctx'), may hold values from -5 to 5
- residual: bfloat16 [4096, 4096], P(('ctx', 'exp')), may hold values from -12 to 12
- out_weight: bfloat16 [4096, 4096], P('exp'), may hold values from -0.25 to 0.25
- norm_gain: float32 [4096], replicated, may hold values from 0.5 to 1.5
- routes: int32 [4096, 8], P(('ctx', 'exp')), may hold values from 0 to 127, as said below
- chosen: int32 [4], replicated, may hold values from 0 to 127, as said below
- block_order: int32 [16], replicated, may hold values from 0 to 15, each once
Outputs:
- stream: bfloat16 [4096, 4096], P(('ctx', 'exp'))
- grams: float32 [4, 4096, 4096], P('exp', 'ctx')
The draws below stay inside these ranges and needn't reach their ends.
Inputs may be any that keep to these rules, and one draw needn't show every extreme that they name: `routes`: each row names 8 different experts. In each aligned block of 128 rows (the rows of one device) no expert is named more than 16 times, and in every block some chosen expert is named exactly 16 times. `chosen`: 4 different experts, among them expert 0 and expert 128 - 1.
All inputs are finite; a program needn't handle non-finite values.
Results may differ from the reference program's by a relative error of at most 0.0085.
Values may be sent and summed in bfloat16 or wider, within the bound.
No kernel may reach another device: no remote copies, remote signals or barrier semaphores. Data moves between devices by JAX's collectives and lax.ppermute only.
A program may use at most 128 MiB of HBM per device.

```python
import jax
import jax.numpy as jnp
from jax import lax

D = 4096
QH = 32
KVH = 2
HD = 128
NE = 128
TOP = 8
SEQ_DEV = 512
BLK = 256
BLOCKS = 16
SEQ = 4096
TOK_DEV = 128
CHOSEN = 4
GROUP = 16
ROWS_MEAN = 256
ROWS_MOST = 512
N_CTX = 8


def shared_chosen(key):
    inner = jax.random.permutation(jax.random.fold_in(key, 88), NE - 2)[:CHOSEN - 2] + 1
    listed = jnp.concatenate([jnp.array([0, NE - 1], dtype=jnp.int32), inner.astype(jnp.int32)])
    return jax.random.permutation(jax.random.fold_in(key, 89), listed).astype(jnp.int32)


def draw_queries(key, part):
    key = jax.random.fold_in(key, 1)
    key_base = jax.random.fold_in(key, 0)
    drawn_vals = jnp.clip(jax.random.normal(key_base, (SEQ, QH * HD), jnp.float32), -4.5, 4.5)
    return drawn_vals.astype(jnp.bfloat16)


def draw_keys(key, part):
    key = jax.random.fold_in(key, 2)
    drawn_vals = jnp.clip(jax.random.normal(key, (SEQ, KVH * HD), jnp.float32), -4.5, 4.5)
    return drawn_vals.astype(jnp.bfloat16)


def draw_residual(key, part):
    key = jax.random.fold_in(key, 3)
    key_base, key_cols, key_rows = jax.random.split(key, 3)
    baseline = jnp.clip(jax.random.normal(key_base, (SEQ, D), jnp.float32), -4.0, 4.0)
    col_scale = jnp.exp(jax.random.uniform(key_cols, (1, D), jnp.float32, jnp.log(0.1), 0.0))
    row_scale = jnp.exp(jax.random.uniform(key_rows, (SEQ, 1), jnp.float32, jnp.log(0.3), jnp.log(3.0)))
    return (baseline * col_scale * row_scale).astype(jnp.bfloat16)


def route_block(key, target):
    mean_load = TOK_DEV * TOP // NE
    key_hot, key_order, key_rows = jax.random.split(key, 3)
    hot_count = jax.random.randint(key_hot, (), NE // 16, 5 * NE // 16)
    rank_ids = jnp.arange(NE)
    counts = jnp.where(rank_ids < hot_count, 2 * mean_load, jnp.where(rank_ids < 2 * hot_count, 0, mean_load))
    expert_order = jax.random.permutation(key_order, NE).astype(jnp.int32)
    where_target = jnp.argmax(expert_order == target)
    expert_order = expert_order.at[where_target].set(expert_order[0]).at[0].set(target)
    run_ends = jnp.cumsum(counts)
    slot_ids = jnp.arange(TOK_DEV * TOP)
    slot_rank = jnp.sum(slot_ids[:, None] >= run_ends[None, :], axis=1)
    listed = expert_order[slot_rank]
    route_table = listed.reshape(TOP, TOK_DEV).T
    row_perm = jax.random.permutation(key_rows, TOK_DEV)
    return route_table[row_perm]


def draw_routes(key, part):
    chosen = shared_chosen(key)
    key = jax.random.fold_in(key, 4)
    key_target, key_blocks = jax.random.split(key)
    target = chosen[jax.random.randint(key_target, (), 0, CHOSEN)]
    block_keys = jax.random.split(key_blocks, SEQ // TOK_DEV)
    tables = jax.vmap(lambda block_key: route_block(block_key, target))(block_keys)
    return tables.reshape(SEQ, TOP).astype(jnp.int32)


def draw_chosen(key, part):
    return shared_chosen(key)


def levels(rng, shape, cuts, low, largest):
    gain, own = 1.0, jax.random.fold_in(rng, 6)
    for position, blocks in cuts:
        steps = jnp.exp(jax.random.uniform(jax.random.fold_in(own, position), (blocks,), jnp.float32, low / len(cuts), largest / len(cuts)))
        gain = gain * jnp.repeat(steps, shape[position] // blocks).reshape([-1 if axis == position else 1 for axis in range(len(shape))])
    return gain


def scatter_about(rng, dims, scale, limit, cuts=(), kind=jnp.bfloat16):
    loudness = levels(rng, dims, cuts, -0.22, 0.18) if cuts else 1.0
    entries = jax.random.normal(rng, dims, jnp.float32) * scale * loudness
    return jnp.minimum(jnp.maximum(entries, -limit), limit).astype(kind)


def setup_inputs(seed: int = 0) -> dict:
    arg_keys = jax.random.split(jax.random.key(seed), 10)
    queries = draw_queries(jax.random.fold_in(arg_keys[9], 71), 0)
    keys = draw_keys(jax.random.fold_in(arg_keys[9], 71), 0)
    values = scatter_about(arg_keys[2], (SEQ, KVH * HD), 1.0, 5.0, ((0, 8),))
    residual = draw_residual(jax.random.fold_in(arg_keys[9], 71), 0)
    out_weight = scatter_about(arg_keys[4], (QH * HD, D), (QH * HD // 8) ** -0.5, 0.25, ((0, 4),))
    norm_gain = jnp.clip(1.0 + 0.1 * jax.random.normal(arg_keys[5], (D,), jnp.float32), 0.5, 1.5)
    routes = draw_routes(jax.random.fold_in(arg_keys[9], 71), 0)
    chosen = draw_chosen(jax.random.fold_in(arg_keys[9], 71), 0)
    block_order = jax.random.permutation(arg_keys[8], BLOCKS).astype(jnp.int32)
    return dict(queries=queries, keys=keys, values=values, residual=residual, out_weight=out_weight, norm_gain=norm_gain, routes=routes, chosen=chosen, block_order=block_order)


def reference(queries, keys, values, residual, out_weight, norm_gain, routes, chosen, block_order):
    token_index = jnp.arange(SEQ, dtype=jnp.int32)
    positions = (block_order[token_index // BLK] * BLK + token_index % BLK).astype(jnp.int32)
    score_scale = 1.0 / HD ** 0.5
    query_heads = queries.reshape(SEQ, QH, HD).transpose(1, 0, 2)
    key_heads = keys.reshape(SEQ, KVH, HD).transpose(1, 0, 2)
    value_heads = values.reshape(SEQ, KVH, HD).transpose(1, 0, 2)

    def head_attention(head_id):
        query_all = query_heads[head_id]
        key_all = key_heads[head_id // GROUP]
        value_all = value_heads[head_id // GROUP]

        def block_attention(block_id):
            query_rows = lax.dynamic_slice_in_dim(query_all, block_id * SEQ_DEV, SEQ_DEV, 0)
            query_pos = lax.dynamic_slice_in_dim(positions, block_id * SEQ_DEV, SEQ_DEV, 0)
            scores = jnp.dot(query_rows, key_all.T, preferred_element_type=jnp.float32) * score_scale
            visible = positions[None, :] <= query_pos[:, None]
            scores = jnp.where(visible, scores, -jnp.inf)
            row_max = lax.optimization_barrier(jnp.max(scores, axis=1, keepdims=True))
            unnormed = jnp.exp(scores - row_max)
            denominator = lax.optimization_barrier(jnp.sum(unnormed, axis=1, keepdims=True))
            weighted = jnp.dot(unnormed.astype(jnp.bfloat16), value_all, preferred_element_type=jnp.float32)
            return (weighted / denominator).astype(jnp.bfloat16)
        return lax.map(block_attention, jnp.arange(N_CTX)).reshape(SEQ, HD)
    attention = lax.map(head_attention, jnp.arange(QH)).transpose(1, 0, 2).reshape(SEQ, QH * HD)
    projection = jnp.dot(attention, out_weight, preferred_element_type=jnp.float32)
    stream = (residual.astype(jnp.float32) + projection).astype(jnp.bfloat16)
    widened = stream.astype(jnp.float32)
    normed = (widened * lax.rsqrt(lax.optimization_barrier(jnp.mean(widened * widened, axis=1, keepdims=True)) + 1e-06) * norm_gain).astype(jnp.bfloat16)
    routed = jnp.any(routes[:, :, None] == chosen[None, None, :], axis=1)

    def expert_gram(expert_slot):
        routed_col = routed[:, expert_slot].astype(jnp.int32)
        row_order = jnp.argsort(1 - routed_col, stable=True)[:ROWS_MOST]
        picked_rows = normed[row_order] * routed_col[row_order][:, None].astype(normed.dtype)
        return jnp.dot(picked_rows.T, picked_rows, preferred_element_type=jnp.float32) / ROWS_MEAN
    grams = lax.map(expert_gram, jnp.arange(CHOSEN))
    return (stream, grams)
```

```python
import functools

import jax
import jax.numpy as jnp
from jax import lax
from jax.experimental import pallas as pl
from jax.experimental.pallas import tpu as pltpu
from jax.sharding import PartitionSpec as P

QH = 32
KVH = 2
HD = 128
NE = 128
TOP = 8
LOG2E = 1.4426950408889634
LOW = -1e30


def swap(block, axis, distance):
    count = lax.axis_size(axis)
    return lax.ppermute(block, axis, [(i, i ^ distance) for i in range(count)])


def gather_ctx(block):
    count = lax.axis_size("ctx")
    half = block.shape[0] // 2
    far = [(0, 0, block)]
    if count == 8:
        along_x, along_y = swap(block, "ctx", 2), swap(block, "ctx", 4)
        far += [(2, 0, along_x), (4, 0, along_y)]
        far += [(6, 0, swap(along_y[:half], "ctx", 2)), (6, half, swap(along_x[half:], "ctx", 4))]
    else:
        distance = 2
        while distance < count:
            far += [(d ^ distance, first, swap(b, "ctx", distance)) for d, first, b in far]
            distance *= 2
    return far + [(d ^ 1, first, swap(b, "ctx", 1)) for d, first, b in far]


def attend_kernel(
    start, block_len, slots_ref, place_ref, dest_ref, query_ref, *refs
):
    n_pieces = len(refs) - 6
    pieces, out_ref = refs[:n_pieces], refs[n_pieces]
    key_ref, value_ref, stacked_ref, top_ref, acc_ref = refs[n_pieces + 1:]
    shards, tokens = dest_ref.shape
    rows = out_ref.shape[0] // shards
    heads = out_ref.shape[1] // HD
    shards_half = shards // 2
    half_rows = shards_half * rows
    stack = heads * half_rows
    step_len = 2 * block_len

    slot = 0
    for piece in pieces:
        for part in range(piece.shape[0] // block_len):
            at = pl.ds(pl.multiple_of(slots_ref[slot] * block_len, block_len), block_len)
            block = piece[part * block_len:(part + 1) * block_len, :]
            key_ref[at, :HD] = block[:, :HD]
            key_ref[at, HD:] = block[:, :HD]
            value_ref[at, :HD] = block[:, HD:]
            slot += 1
    value_ref[:, HD:] = jnp.ones((value_ref.shape[0], HD), jnp.bfloat16)

    for half in range(2):
        place = place_ref[half]
        offsets = []
        for s in range(shards_half):
            shard = half * shards_half + s
            picked = dest_ref[shard:shard + 1, :] == start + lax.broadcasted_iota(
                jnp.int32, (rows, tokens), 0
            )
            token = lax.broadcasted_iota(jnp.int32, (rows, tokens), 1)
            offsets.append(
                jnp.sum(jnp.where(picked, token, 0), axis=1, keepdims=True) + s * tokens
            )
            chosen_rows = jnp.dot(
                picked.astype(jnp.bfloat16),
                query_ref[shard * tokens:(shard + 1) * tokens, :],
                preferred_element_type=jnp.float32,
            ) * (LOG2E / HD ** 0.5)
            high = chosen_rows.astype(jnp.bfloat16)
            low = (chosen_rows - high.astype(jnp.float32)).astype(jnp.bfloat16)
            for h in range(heads):
                at = pl.ds(h * half_rows + s * rows, rows)
                stacked_ref[at, :HD] = high[:, h * HD:(h + 1) * HD]
                stacked_ref[at, HD:] = low[:, h * HD:(h + 1) * HD]
        offset = jnp.concatenate(offsets, axis=0)
        query_place = place * block_len + offset
        top_ref[...] = jnp.full(top_ref.shape, LOW, jnp.float32)
        acc_ref[...] = jnp.zeros(acc_ref.shape, jnp.float32)
        tile_heads = max(1, min(heads, 256 // half_rows))
        tile = tile_heads * half_rows

        def absorb(step, masked):
            at = pl.ds(pl.multiple_of(step * step_len, step_len), step_len)
            key_now, value_now = key_ref[at, :], value_ref[at, :]
            if masked:
                key_place = step * step_len + lax.broadcasted_iota(
                    jnp.int32, (half_rows, step_len), 1
                )
                hidden = jnp.where(key_place <= query_place, 0.0, LOW)
                hidden = jnp.concatenate([hidden] * tile_heads, axis=0)
            for t in range(stack // tile):
                here = pl.ds(t * tile, tile)
                scores = lax.dot_general(
                    stacked_ref[here, :], key_now, (((1,), (1,)), ((), ())),
                    preferred_element_type=jnp.float32,
                )
                if masked:
                    scores = scores + hidden
                top = top_ref[here, :]
                new_top = jnp.maximum(top, jnp.max(scores, axis=1, keepdims=True))
                shrink = jnp.exp2(top - new_top)
                unnormed = jnp.exp2(scores - new_top[:, :1]).astype(jnp.bfloat16)
                added = jnp.dot(unnormed, value_now, preferred_element_type=jnp.float32)
                acc_ref[here, :] = acc_ref[here, :] * shrink[:, :1] + added
                top_ref[here, :] = new_top

        lax.fori_loop(0, place // 2, lambda step, _: absorb(step, False), None)
        absorb(place // 2, True)
        for h in range(heads):
            here = pl.ds(h * half_rows, half_rows)
            out_ref[half * half_rows:(half + 1) * half_rows, h * HD:(h + 1) * HD] = (
                acc_ref[here, :HD] / acc_ref[here, HD:]
            ).astype(jnp.bfloat16)


def attend(start, rows, queries, dest, slots, places, pieces, seq):
    shards, tokens = dest.shape
    local_len, width = queries.shape
    block_len = local_len // 2
    half_rows = shards // 2 * rows
    stack = width // HD * half_rows
    smem = pl.BlockSpec(memory_space=pltpu.SMEM)
    vmem = pl.BlockSpec(memory_space=pltpu.VMEM)
    return pl.pallas_call(
        functools.partial(attend_kernel, start, block_len),
        out_shape=jax.ShapeDtypeStruct((shards * rows, width), jnp.bfloat16),
        in_specs=[smem, smem, vmem, vmem] + [vmem] * len(pieces),
        out_specs=vmem,
        scratch_shapes=[
            pltpu.VMEM((seq, 2 * HD), jnp.bfloat16),
            pltpu.VMEM((seq, 2 * HD), jnp.bfloat16),
            pltpu.VMEM((stack, 2 * HD), jnp.bfloat16),
            pltpu.VMEM((stack, HD), jnp.float32),
            pltpu.VMEM((stack, 2 * HD), jnp.float32),
        ],
        compiler_params=pltpu.CompilerParams(vmem_limit_bytes=48 * 1024 * 1024),
        cost_estimate=pl.CostEstimate(
            flops=4 * stack * 2 * seq * HD, bytes_accessed=6 * 1024 * 1024,
            transcendentals=stack * seq,
        ),
    )(slots, places, dest, queries, *pieces)


def scatter_sum(parts_of, column, order):
    bits = len(order)
    keep_axes = {}
    total = None
    for turn, bit in enumerate(order):
        mine = (column >> bit) & 1
        axis = bits - 1 - bit
        if turn == 0:
            send = parts_of(axis, 1 - mine)
            keep = parts_of(axis, mine)
            live = [b for b in range(bits - 1, -1, -1) if b != bit]
        else:
            axis = live.index(bit)
            send = lax.dynamic_index_in_dim(total, 1 - mine, axis, keepdims=False)
            send = send.astype(jnp.bfloat16)
            keep = lax.dynamic_index_in_dim(total, mine, axis, keepdims=False)
            live.remove(bit)
        came = swap(send, "exp", 1 << bit)
        total = keep.astype(jnp.float32) + came.astype(jnp.float32)
    return total


def local(queries, keys, values, residual, out_weight, norm_gain, routes, chosen, block_order):
    ctx_count = lax.axis_size("ctx")
    ctx_rank = lax.axis_index("ctx")
    exp_count = lax.axis_size("exp")
    column = lax.axis_index("exp")
    local_len = queries.shape[0]
    block_len = local_len // 2
    seq = ctx_count * local_len
    heads_here = queries.shape[1] // HD
    token_rows, features = residual.shape
    n_chosen = chosen.shape[0]
    capacity = 2 * token_rows * TOP // NE

    kv_head = column * heads_here // (QH // KVH)
    key_mine = lax.dynamic_slice_in_dim(keys, kv_head * HD, HD, 1)
    value_mine = lax.dynamic_slice_in_dim(values, kv_head * HD, HD, 1)
    gathered = gather_ctx(jnp.concatenate([key_mine, value_mine], axis=1))
    pieces = [piece for _, _, piece in gathered]
    blocks = [
        (distance, first // block_len + part)
        for distance, first, piece in gathered
        for part in range(piece.shape[0] // block_len)
    ]
    owners = jnp.array([distance for distance, _ in blocks], jnp.int32) ^ ctx_rank
    slots = block_order[2 * owners + jnp.array([part for _, part in blocks], jnp.int32)]
    places = lax.dynamic_slice_in_dim(block_order, 2 * ctx_rank, 2, 0)

    routed = jnp.any(routes[:, :, None] == chosen[None, None, :], axis=1)
    named = jnp.any(routed, axis=1).astype(jnp.int32)
    dest = jnp.where(
        named == 1, jnp.cumsum(named) - 1, jnp.sum(named) + jnp.cumsum(1 - named) - 1
    ).astype(jnp.int32)
    shards = dest[None]
    for bit in range(exp_count.bit_length() - 1):
        came = swap(shards, "exp", 1 << bit)
        upper = (column >> bit) & 1
        shards = jnp.where(
            upper == 1, jnp.concatenate([came, shards]), jnp.concatenate([shards, came])
        )
    order = (dest[None, :] == jnp.arange(token_rows, dtype=jnp.int32)[:, None]).astype(
        jnp.bfloat16
    )

    first_rows = min(token_rows, -(-n_chosen * capacity // 16) * 16)
    chunks = [(0, first_rows)]
    if first_rows < token_rows:
        chunks.append((first_rows, token_rows - first_rows))
    bits = exp_count.bit_length() - 1
    residual_ordered = jnp.dot(order, residual, preferred_element_type=jnp.float32)
    half = features // 2
    streams = []
    for start, rows in chunks:
        attention = attend(start, rows, queries, shards, slots, places, pieces, seq)
        attention = attention.reshape((2,) * bits + (rows, heads_here * HD))

        def parts_of(columns, axis, index):
            picked = lax.dynamic_index_in_dim(attention, index, axis, keepdims=False)
            return jnp.einsum(
                "...rk,kd->...rd", picked, out_weight[:, columns * half:(columns + 1) * half],
                preferred_element_type=jnp.float32,
            ).astype(jnp.bfloat16)

        ways = (list(range(bits)), list(range(bits - 1, -1, -1)))
        projection = jnp.concatenate(
            [
                scatter_sum(functools.partial(parts_of, columns), column, ways[columns])
                for columns in range(2)
            ],
            axis=1,
        )
        streams.append((residual_ordered[start:start + rows] + projection).astype(jnp.bfloat16))
    stream = jnp.dot(
        order.T, jnp.concatenate(streams, axis=0), preferred_element_type=jnp.float32
    ).astype(jnp.bfloat16)

    widened = streams[0].astype(jnp.float32)
    normed = (
        widened * lax.rsqrt(jnp.mean(widened * widened, axis=1, keepdims=True) + 1e-06) * norm_gain
    ).astype(jnp.bfloat16)
    arrival = jnp.cumsum(routed.astype(jnp.int32), axis=0) - 1
    slot_ids = jnp.arange(capacity, dtype=jnp.int32)
    placing = (routed.T[:, None, :] & (arrival.T[:, None, :] == slot_ids[None, :, None])).astype(
        jnp.bfloat16
    )
    placing = jnp.einsum(
        "est,rt->esr", placing, order[:first_rows], preferred_element_type=jnp.float32
    ).astype(jnp.bfloat16)
    outgoing = jnp.einsum(
        "esr,rd->esd", placing, normed, preferred_element_type=jnp.float32
    ).astype(jnp.bfloat16)
    arrived = [lax.dynamic_index_in_dim(outgoing, column, 0, keepdims=False)]
    for distance in range(1, exp_count):
        arrived.append(
            swap(
                lax.dynamic_index_in_dim(outgoing, column ^ distance, 0, keepdims=False),
                "exp",
                distance,
            )
        )
    rows_mine = jnp.concatenate(arrived, axis=0)
    every = jnp.concatenate([piece for _, _, piece in gather_ctx(rows_mine)], axis=0)
    rows_dev = features // ctx_count
    own_cols = lax.dynamic_slice_in_dim(every, ctx_rank * rows_dev, rows_dev, 1)
    gram = lax.dot_general(
        own_cols, every, (((0,), (0,)), ((), ())), preferred_element_type=jnp.float32
    )
    mean_rows = seq * TOP // NE
    return (stream, (gram / mean_rows)[None])


def solution(mesh):
    in_specs = (
        P("ctx", "exp"),
        P("ctx", None),
        P("ctx", None),
        P(("ctx", "exp"), None),
        P("exp", None),
        P(),
        P(("ctx", "exp"), None),
        P(),
        P(),
    )
    out_specs = (P(("ctx", "exp"), None), P("exp", "ctx", None))
    return jax.shard_map(local, mesh=mesh, in_specs=in_specs, out_specs=out_specs, check_vma=False)
```

```python
import functools

import jax
import jax.numpy as jnp
from jax import lax
from jax.experimental import pallas as pl
from jax.experimental.pallas import tpu as pltpu
from jax.sharding import PartitionSpec as P

QH = 32
KVH = 2
HD = 128
NE = 128
TOP = 8
LOG2E = 1.4426950408889634
LOW = -1e30
TILE = 512
STEP = 4
VMEM_MIB = 24


def swap(block, axis, distance):
    count = lax.axis_size(axis)
    return lax.ppermute(block, axis, [(i, i ^ distance) for i in range(count)])


def gather_ctx(block, direct, rider=()):
    count = lax.axis_size("ctx")
    half = block.shape[0] // 2
    far = [(0, 0, block)]
    if direct:
        far += [(d, 0, swap(block, "ctx", d)) for d in range(2, count, 2)]
    elif count == 8:
        along_x, along_y = swap(block, "ctx", 2), swap(block, "ctx", 4)
        far += [(2, 0, along_x), (4, 0, along_y)]
        far += [(6, 0, swap(along_y[:half], "ctx", 2)), (6, half, swap(along_x[half:], "ctx", 4))]
    else:
        distance = 2
        while distance < count:
            far += [(d ^ distance, first, swap(b, "ctx", distance)) for d, first, b in far]
            distance *= 2
    if rider:
        distance, first, last = far[-1]
        last, rider = lax.optimization_barrier((last, rider))
        far[-1] = (distance, first, last)
    return far + [(d ^ 1, first, swap(b, "ctx", 1)) for d, first, b in far], rider


def places_of(named):
    tokens = named.shape[1]
    before = lax.broadcasted_iota(jnp.int32, (tokens, tokens), 0) < lax.broadcasted_iota(
        jnp.int32, (tokens, tokens), 1
    )
    ahead = jnp.dot(
        named.astype(jnp.bfloat16), before.astype(jnp.bfloat16),
        preferred_element_type=jnp.float32,
    )
    index = lax.broadcasted_iota(jnp.int32, (1, tokens), 1).astype(jnp.float32)
    total = jnp.sum(named, axis=1, keepdims=True)
    return jnp.where(named > 0.5, ahead, total + index - ahead).astype(jnp.int32)


def attend_kernel(
    start, tokens, block_len, blocks, order_ref, rank_ref, query_ref, *refs
):
    shards = query_ref.shape[0] // tokens
    masks, pieces, out_ref = refs[:shards], refs[shards:-7], refs[-7]
    key_ref, value_ref, stacked_ref, top_ref, acc_ref, named_ref = refs[-6:]
    for distance in range(shards):
        named_ref[pl.ds(rank_ref[1] ^ distance, 1), :] = masks[distance][...].astype(jnp.float32)
    rows = out_ref.shape[0] // shards
    heads = out_ref.shape[1] // HD
    shards_half = shards // 2
    half_rows = shards_half * rows
    stack = heads * half_rows
    step_len = STEP * block_len

    slot = 0
    for piece in pieces:
        for part in range(piece.shape[0] // block_len):
            distance, at_owner = blocks[slot]
            place = order_ref[2 * (rank_ref[0] ^ distance) + at_owner]
            at = pl.ds(pl.multiple_of(place * block_len, block_len), block_len)
            block = piece[part * block_len:(part + 1) * block_len, :]
            key_ref[at, :HD] = block[:, :HD]
            key_ref[at, HD:] = block[:, :HD]
            value_ref[at, :HD] = block[:, HD:]
            slot += 1
    value_ref[:, HD:] = jnp.ones((value_ref.shape[0], HD), jnp.bfloat16)

    for half in range(2):
        place = order_ref[2 * rank_ref[0] + half]
        offsets = []
        for s in range(shards_half):
            shard = half * shards_half + s
            picked = places_of(named_ref[shard:shard + 1, :]) == start + lax.broadcasted_iota(
                jnp.int32, (rows, tokens), 0
            )
            token = lax.broadcasted_iota(jnp.int32, (rows, tokens), 1)
            offsets.append(
                jnp.sum(jnp.where(picked, token, 0), axis=1, keepdims=True) + s * tokens
            )
            chosen_rows = jnp.dot(
                picked.astype(jnp.bfloat16),
                query_ref[shard * tokens:(shard + 1) * tokens, :],
                preferred_element_type=jnp.float32,
            ) * (LOG2E / HD ** 0.5)
            high = chosen_rows.astype(jnp.bfloat16)
            low = (chosen_rows - high.astype(jnp.float32)).astype(jnp.bfloat16)
            for h in range(heads):
                at = pl.ds(h * half_rows + s * rows, rows)
                stacked_ref[at, :HD] = high[:, h * HD:(h + 1) * HD]
                stacked_ref[at, HD:] = low[:, h * HD:(h + 1) * HD]
        offset = jnp.concatenate(offsets, axis=0)
        query_place = place * block_len + offset
        tile_heads = max(1, min(heads, TILE // half_rows))
        tile = tile_heads * half_rows
        last = place // STEP
        top_ref[...] = jnp.full(top_ref.shape, LOW, jnp.float32)
        acc_ref[...] = jnp.zeros(acc_ref.shape, jnp.float32)

        def absorb(step, masked):
            at = pl.ds(pl.multiple_of(step * step_len, step_len), step_len)
            key_now, value_now = key_ref[at, :], value_ref[at, :]
            if masked:
                key_place = step * step_len + lax.broadcasted_iota(
                    jnp.int32, (half_rows, step_len), 1
                )
                hidden = jnp.where(key_place <= query_place, 0.0, LOW)
                hidden = jnp.concatenate([hidden] * tile_heads, axis=0)

            def score(t):
                scores = lax.dot_general(
                    stacked_ref[t * tile:(t + 1) * tile, :], key_now, (((1,), (1,)), ((), ())),
                    preferred_element_type=jnp.float32,
                )
                return scores + hidden if masked else scores

            ahead = score(0)
            for t in range(stack // tile):
                scores = ahead
                if t + 1 < stack // tile:
                    ahead = score(t + 1)
                here = pl.ds(t * tile, tile)
                top = top_ref[here, :]
                part = scores[:, :HD]
                for c in range(1, step_len // HD):
                    part = jnp.maximum(part, scores[:, c * HD:(c + 1) * HD])
                new_top = jnp.maximum(top, jnp.max(part, axis=1, keepdims=True))
                shrink = jnp.exp2(top - new_top)
                unnormed = jnp.exp2(
                    scores - jnp.concatenate([new_top] * (step_len // HD), axis=1)
                ).astype(jnp.bfloat16)
                added = jnp.dot(unnormed, value_now, preferred_element_type=jnp.float32)
                acc_ref[here, :] = acc_ref[here, :] * jnp.concatenate([shrink] * 2, axis=1) + added
                top_ref[here, :] = new_top

        lax.fori_loop(0, last, lambda step, _: absorb(step, False), None)
        absorb(last, True)
        for h in range(heads):
            here = pl.ds(h * half_rows, half_rows)
            out_ref[half * half_rows:(half + 1) * half_rows, h * HD:(h + 1) * HD] = (
                acc_ref[here, :HD] / acc_ref[here, HD:]
            ).astype(jnp.bfloat16)


def attend(start, rows, queries, named, block_order, rank, blocks, pieces):
    shards, tokens = len(named), named[0].shape[1]
    local_len, width = queries.shape
    block_len = local_len // 2
    seq = len(blocks) * block_len
    stack = width // HD * (shards // 2) * rows
    smem = pl.BlockSpec(memory_space=pltpu.SMEM)
    vmem = pl.BlockSpec(memory_space=pltpu.VMEM)
    return pl.pallas_call(
        functools.partial(attend_kernel, start, tokens, block_len, blocks),
        out_shape=jax.ShapeDtypeStruct((shards * rows, width), jnp.bfloat16),
        in_specs=[smem, smem, vmem] + [vmem] * (shards + len(pieces)),
        out_specs=vmem,
        scratch_shapes=[
            pltpu.VMEM((seq, 2 * HD), jnp.bfloat16),
            pltpu.VMEM((seq, 2 * HD), jnp.bfloat16),
            pltpu.VMEM((stack, 2 * HD), jnp.bfloat16),
            pltpu.VMEM((stack, HD), jnp.float32),
            pltpu.VMEM((stack, 2 * HD), jnp.float32),
            pltpu.VMEM((shards, tokens), jnp.float32),
        ],
        compiler_params=pltpu.CompilerParams(vmem_limit_bytes=VMEM_MIB * 1024 * 1024),
        cost_estimate=pl.CostEstimate(
            flops=4 * stack * 2 * seq * HD, bytes_accessed=6 * 1024 * 1024,
            transcendentals=stack * seq,
        ),
    )(block_order, rank, queries, *named, *pieces)


def finish_kernel(*refs):
    *sums, residual_ref, gain_ref, placing_ref = refs[:7]
    stream_ref, *outgoing = refs[7:]
    half = residual_ref.shape[1] // 2
    square = 0.0
    for c in range(2):
        at = slice(c * half, (c + 1) * half)
        projection = sums[c][...] + sums[2 + c][...].astype(jnp.float32)
        stream = (residual_ref[:, at].astype(jnp.float32) + projection).astype(jnp.bfloat16)
        stream_ref[:, at] = stream
        widened = stream.astype(jnp.float32)
        square = square + jnp.sum(widened * widened, axis=1, keepdims=True)
    scale = lax.rsqrt(square / (2 * half) + 1e-06)
    rows = outgoing[0].shape[0]
    for first in range(0, 2 * half, 512):
        at = slice(first, first + 512)
        normed = (stream_ref[:, at].astype(jnp.float32) * scale * gain_ref[:, at]).astype(
            jnp.bfloat16
        )
        placed = jnp.dot(placing_ref[...], normed, preferred_element_type=jnp.float32)
        for d, out_ref in enumerate(outgoing):
            out_ref[:, at] = placed[d * rows:(d + 1) * rows].astype(jnp.bfloat16)


def finish(keeps, came, residual, gain, placing, places):
    rows, features = residual.shape
    vmem = pl.BlockSpec(memory_space=pltpu.VMEM)
    out = jax.ShapeDtypeStruct((placing.shape[0] // places, features), jnp.bfloat16)
    return pl.pallas_call(
        finish_kernel,
        out_shape=[jax.ShapeDtypeStruct((rows, features), jnp.bfloat16)] + [out] * places,
        in_specs=[vmem] * 7,
        out_specs=[vmem] * (1 + places),
        compiler_params=pltpu.CompilerParams(vmem_limit_bytes=VMEM_MIB * 1024 * 1024),
    )(*keeps, *came, residual, gain, placing)


def scatter_turn(total, column, bit, axis, after=None):
    mine = (column >> bit) & 1
    send = lax.dynamic_index_in_dim(total, 1 - mine, axis, keepdims=False)
    keep = lax.dynamic_index_in_dim(total, mine, axis, keepdims=False)
    came = swap(send.astype(jnp.bfloat16), "exp", 1 << bit)
    if after is not None:
        came, _ = lax.optimization_barrier((came, after))
    return keep, came


def local(queries, keys, values, residual, out_weight, norm_gain, routes, chosen, block_order):
    ctx_count = lax.axis_size("ctx")
    ctx_rank = lax.axis_index("ctx")
    exp_count = lax.axis_size("exp")
    column = lax.axis_index("exp")
    local_len = queries.shape[0]
    block_len = local_len // 2
    seq = ctx_count * local_len
    heads_here = queries.shape[1] // HD
    token_rows, features = residual.shape
    n_chosen = chosen.shape[0]
    per_exp = n_chosen // exp_count
    capacity = 2 * token_rows * TOP // NE

    kv_head = column * heads_here // (QH // KVH)
    key_mine = lax.dynamic_slice_in_dim(keys, kv_head * HD, HD, 1)
    value_mine = lax.dynamic_slice_in_dim(values, kv_head * HD, HD, 1)
    routed = jnp.any(routes[:, :, None] == chosen[None, None, :], axis=1)
    named = jnp.any(routes[:, :, None] == chosen[None, None, :], axis=(1, 2)).astype(jnp.int32)
    named_all = [named[None]] + [swap(named[None], "exp", d) for d in range(1, exp_count)]
    gathered, named_all = gather_ctx(
        jnp.concatenate([key_mine, value_mine], axis=1), True, named_all
    )
    pieces = [piece for _, _, piece in gathered]
    blocks = [
        (distance, first // block_len + part)
        for distance, first, piece in gathered
        for part in range(piece.shape[0] // block_len)
    ]
    rank = jnp.stack([ctx_rank, column]).astype(jnp.int32)

    dest = places_of(named.astype(jnp.float32)[None])
    order = (dest == jnp.arange(token_rows, dtype=jnp.int32)[:, None]).astype(jnp.bfloat16)

    first_rows = min(token_rows, -(-n_chosen * capacity // 16) * 16)
    chunks = [(0, first_rows)]
    if first_rows < token_rows:
        chunks.append((first_rows, token_rows - first_rows))
    bits = exp_count.bit_length() - 1
    residual_ordered = jnp.dot(order, residual, preferred_element_type=jnp.float32).astype(
        jnp.bfloat16
    )
    half = features // 2
    ways = (list(range(bits)), list(range(bits - 1, -1, -1)))

    def attend_chunk(chunk, queries):
        start, rows = chunk
        attention = attend(start, rows, queries, named_all, block_order, rank, blocks, pieces)
        return attention.reshape((2,) * bits + (rows, heads_here * HD))

    def project(attention, columns, stays):
        bit = ways[columns][0]
        index = ((column >> bit) & 1) ^ (not stays)
        picked = lax.dynamic_index_in_dim(attention, index, bits - 1 - bit, keepdims=False)
        return jnp.einsum(
            "...rk,kd->...rd", picked, out_weight[:, columns * half:(columns + 1) * half],
            preferred_element_type=jnp.float32,
        ).astype(jnp.bfloat16)

    def first_turn(sends):
        return [swap(sends[c], "exp", 1 << ways[c][0]) for c in range(2)]

    def add_first(keeps, came):
        totals = [k.astype(jnp.float32) + c.astype(jnp.float32) for k, c in zip(keeps, came)]
        return lax.optimization_barrier(totals)

    def other_turns(totals):
        keeps, cames = [], []
        for c in range(2):
            keep = totals[c]
            live = [bit for bit in range(bits - 1, -1, -1) if bit != ways[c][0]]
            for turn, bit in enumerate(ways[c][1:]):
                if turn > 0:
                    keep = keep.astype(jnp.float32) + came.astype(jnp.float32)
                keep, came = scatter_turn(keep, column, bit, live.index(bit))
                live.remove(bit)
            keeps.append(keep)
            cames.append(came)
        return keeps, cames

    attention = attend_chunk(chunks[0], queries)
    sends = [project(attention, c, False) for c in range(2)]
    came = first_turn(sends)
    keeps = [project(attention, c, True) for c in range(2)]
    if len(chunks) > 1:
        _, queries = lax.optimization_barrier((sends, queries))
        attention_late = attend_chunk(chunks[1], queries)
        came, attention_late = lax.optimization_barrier((came, attention_late))
    keeps, came = other_turns(add_first(keeps, came))

    arrival = jnp.cumsum(routed.astype(jnp.int32), axis=0) - 1
    slot_ids = jnp.arange(capacity, dtype=jnp.int32)
    placing = (routed.T[:, None, :] & (arrival.T[:, None, :] == slot_ids[None, :, None])).astype(
        jnp.bfloat16
    )
    placing = jnp.einsum(
        "est,rt->esr", placing, order[:first_rows], preferred_element_type=jnp.float32
    ).astype(jnp.bfloat16)
    placing = jnp.concatenate(
        [
            lax.dynamic_slice_in_dim(placing, (column ^ d) * per_exp, per_exp, 0)
            for d in range(exp_count)
        ]
    ).reshape(n_chosen * capacity, first_rows)
    stream_first, *outgoing = finish(
        keeps, came, residual_ordered[:first_rows], norm_gain[None], placing, exp_count
    )
    streams = [stream_first]
    arrived = [outgoing[0]] + [swap(outgoing[d], "exp", d) for d in range(1, exp_count)]
    if len(chunks) > 1:
        _, attention_late = lax.optimization_barrier((outgoing, attention_late))
        sends, keeps = [
            [project(attention_late, c, stays) for c in range(2)] for stays in (False, True)
        ]
        arrived, sends = lax.optimization_barrier((arrived, sends))
        came = first_turn(sends)
    rows_mine = jnp.concatenate(arrived, axis=0)
    every = jnp.concatenate([piece for _, _, piece in gather_ctx(rows_mine, False)[0]], axis=0)
    if len(chunks) > 1:
        came, every = lax.optimization_barrier((came, every))
        keeps, came = other_turns(add_first(keeps, came))
        projection = jnp.concatenate(
            [k.astype(jnp.float32) + c.astype(jnp.float32) for k, c in zip(keeps, came)], axis=1
        )
        streams.append((residual_ordered[first_rows:] + projection).astype(jnp.bfloat16))
    stream = jnp.dot(
        order.T, jnp.concatenate(streams, axis=0), preferred_element_type=jnp.float32
    ).astype(jnp.bfloat16)
    rows_dev = features // ctx_count
    own_cols = lax.dynamic_slice_in_dim(every, ctx_rank * rows_dev, rows_dev, 1)
    gram = lax.dot_general(
        own_cols, every, (((0,), (0,)), ((), ())), preferred_element_type=jnp.float32
    )
    mean_rows = seq * TOP // NE
    return (stream, (gram / mean_rows)[None])


def solution(mesh):
    in_specs = (
        P("ctx", "exp"),
        P("ctx", None),
        P("ctx", None),
        P(("ctx", "exp"), None),
        P("exp", None),
        P(),
        P(("ctx", "exp"), None),
        P(),
        P(),
    )
    out_specs = (P(("ctx", "exp"), None), P("exp", "ctx", None))
    return jax.shard_map(local, mesh=mesh, in_specs=in_specs, out_specs=out_specs, check_vma=False)
```

```python
import functools

import jax
import jax.numpy as jnp
from jax import lax
from jax.experimental import pallas as pl
from jax.experimental.pallas import tpu as pltpu
from jax.sharding import PartitionSpec as P

QH = 32
KVH = 2
HD = 128
NE = 128
TOP = 8
LOG2E = 1.4426950408889634
LOW = -1e30
TILE = 512
STEP = 4
VMEM_MIB = 24


def swap(block, axis, distance):
    count = lax.axis_size(axis)
    return lax.ppermute(block, axis, [(i, i ^ distance) for i in range(count)])


def gather_ctx(block, direct, rider=(), near=None):
    count = lax.axis_size("ctx")
    half = block.shape[0] // 2
    far = [(0, 0, block)]
    if direct:
        far += [(d, 0, swap(block, "ctx", d)) for d in range(2, count, 2)]
    elif count == 8:
        along_x, along_y = swap(block, "ctx", 2), swap(block, "ctx", 4)
        far += [(2, 0, along_x), (4, 0, along_y)]
        far += [(6, 0, swap(along_y[:half], "ctx", 2)), (6, half, swap(along_x[half:], "ctx", 4))]
    else:
        distance = 2
        while distance < count:
            far += [(d ^ distance, first, swap(b, "ctx", distance)) for d, first, b in far]
            distance *= 2
    if near is None:
        late, _ = lax.optimization_barrier((block, far[1][2]))
        near = swap(late, "ctx", 1)
    if rider:
        distance, first, last = far[-1]
        last, rider = lax.optimization_barrier((last, rider))
        far[-1] = (distance, first, last)
    return far + [
        (d ^ 1, first, near if b is block and near is not None else swap(b, "ctx", 1))
        for d, first, b in far
    ], rider


def places_of(named):
    tokens = named.shape[1]
    before = lax.broadcasted_iota(jnp.int32, (tokens, tokens), 0) < lax.broadcasted_iota(
        jnp.int32, (tokens, tokens), 1
    )
    ahead = jnp.dot(
        named.astype(jnp.bfloat16), before.astype(jnp.bfloat16),
        preferred_element_type=jnp.float32,
    )
    index = lax.broadcasted_iota(jnp.int32, (1, tokens), 1).astype(jnp.float32)
    total = jnp.sum(named, axis=1, keepdims=True)
    return jnp.where(named > 0.5, ahead, total + index - ahead).astype(jnp.int32)


def attend_kernel(
    start, tokens, block_len, blocks, order_ref, rank_ref, query_ref, *refs
):
    shards = query_ref.shape[0] // tokens
    masks, pieces, out_ref = refs[:shards], refs[shards:-7], refs[-7]
    key_ref, value_ref, stacked_ref, top_ref, acc_ref, named_ref = refs[-6:]
    for distance in range(shards):
        named_ref[pl.ds(rank_ref[1] ^ distance, 1), :] = masks[distance][...].astype(jnp.float32)
    rows = out_ref.shape[0] // shards
    heads = out_ref.shape[1] // HD
    shards_half = shards // 2
    half_rows = shards_half * rows
    stack = heads * half_rows
    step_len = STEP * block_len

    slot = 0
    for piece in pieces:
        for part in range(piece.shape[0] // block_len):
            distance, at_owner = blocks[slot]
            place = order_ref[2 * (rank_ref[0] ^ distance) + at_owner]
            at = pl.ds(pl.multiple_of(place * block_len, block_len), block_len)
            block = piece[part * block_len:(part + 1) * block_len, :]
            key_ref[at, :HD] = block[:, :HD]
            key_ref[at, HD:] = block[:, :HD]
            value_ref[at, :HD] = block[:, HD:]
            slot += 1
    value_ref[:, HD:] = jnp.ones((value_ref.shape[0], HD), jnp.bfloat16)

    for half in range(2):
        place = order_ref[2 * rank_ref[0] + half]
        offsets = []
        for s in range(shards_half):
            shard = half * shards_half + s
            picked = places_of(named_ref[shard:shard + 1, :]) == start + lax.broadcasted_iota(
                jnp.int32, (rows, tokens), 0
            )
            token = lax.broadcasted_iota(jnp.int32, (rows, tokens), 1)
            offsets.append(
                jnp.sum(jnp.where(picked, token, 0), axis=1, keepdims=True) + s * tokens
            )
            chosen_rows = jnp.dot(
                picked.astype(jnp.bfloat16),
                query_ref[shard * tokens:(shard + 1) * tokens, :],
                preferred_element_type=jnp.float32,
            ) * (LOG2E / HD ** 0.5)
            high = chosen_rows.astype(jnp.bfloat16)
            low = (chosen_rows - high.astype(jnp.float32)).astype(jnp.bfloat16)
            for h in range(heads):
                at = pl.ds(h * half_rows + s * rows, rows)
                stacked_ref[at, :HD] = high[:, h * HD:(h + 1) * HD]
                stacked_ref[at, HD:] = low[:, h * HD:(h + 1) * HD]
        offset = jnp.concatenate(offsets, axis=0)
        query_place = place * block_len + offset
        tile_heads = max(1, min(heads, TILE // half_rows))
        tile = tile_heads * half_rows
        last = place // STEP
        top_ref[...] = jnp.full(top_ref.shape, LOW, jnp.float32)
        acc_ref[...] = jnp.zeros(acc_ref.shape, jnp.float32)

        def absorb(step, masked):
            at = pl.ds(pl.multiple_of(step * step_len, step_len), step_len)
            key_now, value_now = key_ref[at, :], value_ref[at, :]
            if masked:
                key_place = step * step_len + lax.broadcasted_iota(
                    jnp.int32, (half_rows, step_len), 1
                )
                hidden = jnp.where(key_place <= query_place, 0.0, LOW)
                hidden = jnp.concatenate([hidden] * tile_heads, axis=0)

            def score(t):
                scores = lax.dot_general(
                    stacked_ref[t * tile:(t + 1) * tile, :], key_now, (((1,), (1,)), ((), ())),
                    preferred_element_type=jnp.float32,
                )
                return scores + hidden if masked else scores

            ahead = score(0)
            for t in range(stack // tile):
                scores = ahead
                if t + 1 < stack // tile:
                    ahead = score(t + 1)
                here = pl.ds(t * tile, tile)
                top = top_ref[here, :]
                part = scores[:, :HD]
                for c in range(1, step_len // HD):
                    part = jnp.maximum(part, scores[:, c * HD:(c + 1) * HD])
                new_top = jnp.maximum(top, jnp.max(part, axis=1, keepdims=True))
                shrink = jnp.exp2(top - new_top)
                unnormed = jnp.exp2(
                    scores - jnp.concatenate([new_top] * (step_len // HD), axis=1)
                ).astype(jnp.bfloat16)
                added = jnp.dot(unnormed, value_now, preferred_element_type=jnp.float32)
                acc_ref[here, :] = acc_ref[here, :] * jnp.concatenate([shrink] * 2, axis=1) + added
                top_ref[here, :] = new_top

        lax.fori_loop(0, last, lambda step, _: absorb(step, False), None)
        absorb(last, True)
        for h in range(heads):
            here = pl.ds(h * half_rows, half_rows)
            out_ref[half * half_rows:(half + 1) * half_rows, h * HD:(h + 1) * HD] = (
                acc_ref[here, :HD] / acc_ref[here, HD:]
            ).astype(jnp.bfloat16)


def attend(start, rows, queries, named, block_order, rank, blocks, pieces):
    shards, tokens = len(named), named[0].shape[1]
    local_len, width = queries.shape
    block_len = local_len // 2
    seq = len(blocks) * block_len
    stack = width // HD * (shards // 2) * rows
    smem = pl.BlockSpec(memory_space=pltpu.SMEM)
    vmem = pl.BlockSpec(memory_space=pltpu.VMEM)
    return pl.pallas_call(
        functools.partial(attend_kernel, start, tokens, block_len, blocks),
        out_shape=jax.ShapeDtypeStruct((shards * rows, width), jnp.bfloat16),
        in_specs=[smem, smem, vmem] + [vmem] * (shards + len(pieces)),
        out_specs=vmem,
        scratch_shapes=[
            pltpu.VMEM((seq, 2 * HD), jnp.bfloat16),
            pltpu.VMEM((seq, 2 * HD), jnp.bfloat16),
            pltpu.VMEM((stack, 2 * HD), jnp.bfloat16),
            pltpu.VMEM((stack, HD), jnp.float32),
            pltpu.VMEM((stack, 2 * HD), jnp.float32),
            pltpu.VMEM((shards, tokens), jnp.float32),
        ],
        compiler_params=pltpu.CompilerParams(vmem_limit_bytes=VMEM_MIB * 1024 * 1024),
        cost_estimate=pl.CostEstimate(
            flops=4 * stack * 2 * seq * HD, bytes_accessed=6 * 1024 * 1024,
            transcendentals=stack * seq,
        ),
    )(block_order, rank, queries, *named, *pieces)


def finish_kernel(*refs):
    *sums, residual_ref, gain_ref, placing_ref = refs[:7]
    stream_ref, *outgoing = refs[7:]
    half = residual_ref.shape[1] // 2
    square = 0.0
    for c in range(2):
        at = slice(c * half, (c + 1) * half)
        projection = sums[c][...] + sums[2 + c][...].astype(jnp.float32)
        stream = (residual_ref[:, at].astype(jnp.float32) + projection).astype(jnp.bfloat16)
        stream_ref[:, at] = stream
        widened = stream.astype(jnp.float32)
        square = square + jnp.sum(widened * widened, axis=1, keepdims=True)
    scale = lax.rsqrt(square / (2 * half) + 1e-06)
    rows = outgoing[0].shape[0]
    for first in range(0, 2 * half, 512):
        at = slice(first, first + 512)
        normed = (stream_ref[:, at].astype(jnp.float32) * scale * gain_ref[:, at]).astype(
            jnp.bfloat16
        )
        placed = jnp.dot(placing_ref[...], normed, preferred_element_type=jnp.float32)
        for d, out_ref in enumerate(outgoing):
            out_ref[:, at] = placed[d * rows:(d + 1) * rows].astype(jnp.bfloat16)


def finish(keeps, came, residual, gain, placing, places):
    rows, features = residual.shape
    vmem = pl.BlockSpec(memory_space=pltpu.VMEM)
    out = jax.ShapeDtypeStruct((placing.shape[0] // places, features), jnp.bfloat16)
    return pl.pallas_call(
        finish_kernel,
        out_shape=[jax.ShapeDtypeStruct((rows, features), jnp.bfloat16)] + [out] * places,
        in_specs=[vmem] * 7,
        out_specs=[vmem] * (1 + places),
        compiler_params=pltpu.CompilerParams(vmem_limit_bytes=VMEM_MIB * 1024 * 1024),
    )(*keeps, *came, residual, gain, placing)


def scatter_turn(total, column, bit, axis, after=None):
    mine = (column >> bit) & 1
    send = lax.dynamic_index_in_dim(total, 1 - mine, axis, keepdims=False)
    keep = lax.dynamic_index_in_dim(total, mine, axis, keepdims=False)
    came = swap(send.astype(jnp.bfloat16), "exp", 1 << bit)
    if after is not None:
        came, _ = lax.optimization_barrier((came, after))
    return keep, came


def local(queries, keys, values, residual, out_weight, norm_gain, routes, chosen, block_order):
    ctx_count = lax.axis_size("ctx")
    ctx_rank = lax.axis_index("ctx")
    exp_count = lax.axis_size("exp")
    column = lax.axis_index("exp")
    local_len = queries.shape[0]
    block_len = local_len // 2
    seq = ctx_count * local_len
    heads_here = queries.shape[1] // HD
    token_rows, features = residual.shape
    n_chosen = chosen.shape[0]
    per_exp = n_chosen // exp_count
    capacity = 2 * token_rows * TOP // NE

    kv_head = column * heads_here // (QH // KVH)
    key_mine = lax.dynamic_slice_in_dim(keys, kv_head * HD, HD, 1)
    value_mine = lax.dynamic_slice_in_dim(values, kv_head * HD, HD, 1)
    kv_pair = jnp.concatenate([key_mine, value_mine], axis=1)
    kv_near = swap(kv_pair, "ctx", 1)
    kv_near, routes = lax.optimization_barrier((kv_near, routes))
    routed = jnp.any(routes[:, :, None] == chosen[None, None, :], axis=1)
    named = jnp.any(routes[:, :, None] == chosen[None, None, :], axis=(1, 2)).astype(jnp.int32)
    named_all = [named[None]] + [swap(named[None], "exp", d) for d in range(1, exp_count)]
    gathered, named_all = gather_ctx(kv_pair, True, named_all, near=kv_near)
    pieces = [piece for _, _, piece in gathered]
    blocks = [
        (distance, first // block_len + part)
        for distance, first, piece in gathered
        for part in range(piece.shape[0] // block_len)
    ]
    rank = jnp.stack([ctx_rank, column]).astype(jnp.int32)

    dest = places_of(named.astype(jnp.float32)[None])
    order = (dest == jnp.arange(token_rows, dtype=jnp.int32)[:, None]).astype(jnp.bfloat16)

    first_rows = min(token_rows, -(-n_chosen * capacity // 16) * 16)
    chunks = [(0, first_rows)]
    if first_rows < token_rows:
        chunks.append((first_rows, token_rows - first_rows))
    bits = exp_count.bit_length() - 1
    half = features // 2
    ways = (list(range(bits)), list(range(bits - 1, -1, -1)))

    def attend_chunk(chunk, queries):
        start, rows = chunk
        attention = attend(start, rows, queries, named_all, block_order, rank, blocks, pieces)
        return attention.reshape((2,) * bits + (rows, heads_here * HD))

    def project(attention, columns, stays):
        bit = ways[columns][0]
        index = ((column >> bit) & 1) ^ (not stays)
        picked = lax.dynamic_index_in_dim(attention, index, bits - 1 - bit, keepdims=False)
        return jnp.einsum(
            "...rk,kd->...rd", picked, out_weight[:, columns * half:(columns + 1) * half],
            preferred_element_type=jnp.float32,
        ).astype(jnp.bfloat16)

    def first_turn(sends):
        return [swap(sends[c], "exp", 1 << ways[c][0]) for c in range(2)]

    def add_first(keeps, came):
        totals = [k.astype(jnp.float32) + c.astype(jnp.float32) for k, c in zip(keeps, came)]
        return lax.optimization_barrier(totals)

    def other_turns(totals):
        keeps, cames = [], []
        for c in range(2):
            keep = totals[c]
            live = [bit for bit in range(bits - 1, -1, -1) if bit != ways[c][0]]
            for turn, bit in enumerate(ways[c][1:]):
                if turn > 0:
                    keep = keep.astype(jnp.float32) + came.astype(jnp.float32)
                keep, came = scatter_turn(keep, column, bit, live.index(bit))
                live.remove(bit)
            keeps.append(keep)
            cames.append(came)
        return keeps, cames

    attention = attend_chunk(chunks[0], queries)
    sends = [project(attention, c, False) for c in range(2)]
    came = first_turn(sends)
    keeps = [project(attention, c, True) for c in range(2)]
    _, residual = lax.optimization_barrier((sends, residual))
    residual_ordered = jnp.dot(order, residual, preferred_element_type=jnp.float32).astype(
        jnp.bfloat16
    )
    if len(chunks) > 1:
        _, queries = lax.optimization_barrier((sends, queries))
        attention_late = attend_chunk(chunks[1], queries)
        came, keeps, attention_late = lax.optimization_barrier((came, keeps, attention_late))
    keeps, came = other_turns(add_first(keeps, came))

    arrival = jnp.cumsum(routed.astype(jnp.int32), axis=0) - 1
    slot_ids = jnp.arange(capacity, dtype=jnp.int32)
    placing = (routed.T[:, None, :] & (arrival.T[:, None, :] == slot_ids[None, :, None])).astype(
        jnp.bfloat16
    )
    placing = jnp.einsum(
        "est,rt->esr", placing, order[:first_rows], preferred_element_type=jnp.float32
    ).astype(jnp.bfloat16)
    placing = jnp.concatenate(
        [
            lax.dynamic_slice_in_dim(placing, (column ^ d) * per_exp, per_exp, 0)
            for d in range(exp_count)
        ]
    ).reshape(n_chosen * capacity, first_rows)
    stream_first, *outgoing = finish(
        keeps, came, residual_ordered[:first_rows], norm_gain[None], placing, exp_count
    )
    streams = [stream_first]
    arrived = [outgoing[0]] + [swap(outgoing[d], "exp", d) for d in range(1, exp_count)]
    if len(chunks) > 1:
        _, attention_late = lax.optimization_barrier((outgoing, attention_late))
        sends, keeps = [
            [project(attention_late, c, stays) for c in range(2)] for stays in (False, True)
        ]
        arrived, sends = lax.optimization_barrier((arrived, sends))
        came = first_turn(sends)
    rows_mine = jnp.concatenate(arrived, axis=0)
    every = jnp.concatenate([piece for _, _, piece in gather_ctx(rows_mine, False)[0]], axis=0)
    if len(chunks) > 1:
        came, every = lax.optimization_barrier((came, every))
        keeps, came = other_turns(add_first(keeps, came))
        projection = jnp.concatenate(
            [k.astype(jnp.float32) + c.astype(jnp.float32) for k, c in zip(keeps, came)], axis=1
        )
        streams.append((residual_ordered[first_rows:] + projection).astype(jnp.bfloat16))
    stream = jnp.dot(
        order.T, jnp.concatenate(streams, axis=0), preferred_element_type=jnp.float32
    ).astype(jnp.bfloat16)
    rows_dev = features // ctx_count
    own_cols = lax.dynamic_slice_in_dim(every, ctx_rank * rows_dev, rows_dev, 1)
    gram = lax.dot_general(
        own_cols, every, (((0,), (0,)), ((), ())), preferred_element_type=jnp.float32
    )
    mean_rows = seq * TOP // NE
    return (stream, (gram / mean_rows)[None])


def solution(mesh):
    in_specs = (
        P("ctx", "exp"),
        P("ctx", None),
        P("ctx", None),
        P(("ctx", "exp"), None),
        P("exp", None),
        P(),
        P(("ctx", "exp"), None),
        P(),
        P(),
    )
    out_specs = (P(("ctx", "exp"), None), P("exp", "ctx", None))
    return jax.shard_map(local, mesh=mesh, in_specs=in_specs, out_specs=out_specs, check_vma=False)
```
